512 devices in a mesh: outer: 32 (over x_lo, z), dev: 16 (over x_hi, y, core).
Axes of the slice: x: 4 (x_hi: 2, x_lo: 2; x = x_hi * 2 + x_lo), y: 4, z: 16, core: 2. Of those that a mesh axis runs over, the one named last changes fastest.
Arguments:
- grads: float32 [32, 16, 1048576], P('outer', 'dev'), may hold values from -6 to 6
- residual: float32 [32, 1048576], P('outer', 'dev'), may hold values from -24 to 24
- sign_bits: int32 [1024], replicated, may hold values from 0 to 1
- kept_index: int32 [1024], replicated, may hold values from 0 to 7
Outputs:
- synced: float32 [1048576], replicated
- new_residual: float32 [32, 1048576], P('outer', 'dev')
The draws below stay inside these ranges and needn't reach their ends.
All inputs are finite; a program needn't handle non-finite values.
Results may differ from the reference program's by a relative error of at most 0.000073.
Values sent between devices are 32-bit elements; how exact they have to be, the bound alone decides.
A program may use at most 64 MiB of HBM per device.

```python
import math
import jax
import jax.numpy as jnp
import numpy as np
from jax import lax

HAD = 1024
KEEP = 128
BLOCKS = 1024
BUCKET = 1048576
N_OUTER = 32
N_DEV = 16


def touch_ends(drawn, rng, smallest, high):
    extent = drawn.shape
    place = [jax.random.randint(jax.random.fold_in(rng, axis), (), 0, extent[axis]) for axis in range(len(extent))]
    drawn = drawn.at[tuple(place)].set(smallest)
    longest = extent.index(max(extent))
    place[longest] = (place[longest] + 1) % extent[longest]
    return drawn.at[tuple(place)].set(high)


def raised(values, key, source, target, blocks, factor):
    owner, partner = [(jnp.arange(values.shape[dim]) // (values.shape[dim] // blocks)).reshape([-1 if axis == dim else 1 for axis in range(values.ndim)]) for dim in (source, target)]
    chosen = jax.random.permutation(key, blocks)[partner]
    strong = (owner == chosen) | (owner == (partner + blocks // 2) % blocks)
    return jnp.where(strong, factor * values, values)


def shard_levels(own_key, dims, split, least, top_value):
    loudness, own = 1.0, jax.random.fold_in(own_key, 6)
    for axis_at, parts in split:
        heights = jnp.exp(jax.random.uniform(jax.random.fold_in(own, axis_at), (parts,), jnp.float32, least / len(split), top_value / len(split)))
        loudness = loudness * jnp.repeat(heights, dims[axis_at] // parts).reshape([-1 if axis == axis_at else 1 for axis in range(len(dims))])
    return loudness


def bell_draw(own_key, dims, deviation, limit, shards=(), kind=jnp.bfloat16):
    result = deviation * jax.random.normal(own_key, dims, jnp.float32)
    if shards:
        result = result * shard_levels(own_key, dims, shards, -0.22, 0.18)
    return jnp.clip(result, -limit, limit).astype(kind)


def bell_draw_with(stream_key, dims, scale, reach, shards, heavy, held_as=jnp.bfloat16):
    values = scale * jax.random.normal(stream_key, dims, jnp.float32)
    if shards:
        values = values * shard_levels(stream_key, dims, shards, -0.22, 0.18)
    return jnp.clip(raised(values, jax.random.fold_in(stream_key, 3), *heavy), -reach, reach).astype(held_as)


def setup_inputs(seed: int = 0) -> dict:
    key_list = jax.random.split(jax.random.key(seed), 5)
    grads = bell_draw_with(key_list[0], (N_OUTER, N_DEV, BUCKET), 1.0, 6.0, ((0, 32), (1, 16)), (1, 2, 16, 2.0), jnp.float32)
    residual = bell_draw(key_list[1], (N_OUTER, BUCKET), 4.0, 24.0, ((0, 32), (1, 16)), jnp.float32)
    sign_bits = touch_ends(jax.random.randint(key_list[2], (HAD,), 0, 2), jax.random.fold_in(key_list[2], 1), 0, 1).astype(jnp.int32)
    kept_index = touch_ends(jax.random.randint(key_list[3], (BLOCKS,), 0, 8), jax.random.fold_in(key_list[3], 1), 0, 7).astype(jnp.int32)
    return {"grads": grads, "residual": residual, "sign_bits": sign_bits, "kept_index": kept_index}


def hadamard_table():
    index = np.arange(HAD)
    common = index[:, None] & index[None, :]
    parity = np.zeros((HAD, HAD), np.int64)
    for bit in range(HAD.bit_length()):
        parity = parity ^ common >> bit & 1
    return jnp.asarray(((1 - 2 * parity) / math.sqrt(HAD)).astype(np.float32))

def select_runs(values, picks):
    onehot = (picks[:, None] == jnp.arange(8, dtype=jnp.int32)[None, :]).astype(jnp.float32)
    return lax.optimization_barrier(jnp.sum(values.reshape(-1, 8, KEEP) * onehot[:, :, None], axis=1))

def decode_runs(sketch, picks, sign_vec, table):
    onehot = (picks[:, None] == jnp.arange(8, dtype=jnp.int32)[None, :]).astype(jnp.float32)
    placed = (sketch[:, None, :] * onehot[:, :, None]).reshape(-1, HAD)
    return (jnp.dot(placed, table, precision=lax.Precision.HIGHEST) * sign_vec[None, :]).reshape(-1)

def reference(grads, residual, sign_bits, kept_index):
    table = hadamard_table()
    sign_vec = (1 - 2 * sign_bits).astype(jnp.float32)
    pod_sum = lax.optimization_barrier(jnp.sum(grads, axis=1))
    corrected = pod_sum + residual

    def one_pod(row):
        blocks = row.reshape(-1, HAD) * sign_vec[None, :]
        spread = jnp.dot(blocks, table, precision=lax.Precision.HIGHEST)
        kept = select_runs(spread, kept_index)
        return (kept, row - decode_runs(kept, kept_index, sign_vec, table))
    kept, new_residual = lax.map(one_pod, corrected)
    total = lax.optimization_barrier(jnp.sum(kept, axis=0))
    synced = decode_runs(total, kept_index, sign_vec, table) / N_OUTER
    return (synced, new_residual)
```

```python
import jax
import jax.numpy as jnp
from jax import lax
from jax.experimental import pallas as pl
from jax.experimental.pallas import tpu as pltpu
from jax.sharding import PartitionSpec as P

MESH = pl.DeviceIdType.MESH
F32 = jnp.float32
LANES = 128
SHARD = 512
CHUNK = 16
FIRST = 208


def place():
    o, d = lax.axis_index("outer"), lax.axis_index("dev")
    x = (d // 8) * 2 + o // 16
    return x, (d // 2) % 4, (o % 16) // 2, o % 2, d % 2


def device(x, y, zg, zp, c):
    return ((x % 2) * 16 + zg * 2 + zp, (x // 2) * 8 + y * 2 + c)


def rows(start, size, multiple):
    return pl.ds(pl.multiple_of(start, multiple), size)


def spread_index(row):
    return jnp.transpose(jnp.broadcast_to(row.astype(F32), (LANES, LANES))).astype(jnp.int32)


def flips(k):
    return [(1 - 2 * ((k >> bit) & 1)).astype(F32) for bit in range(3)]


def fold(t, s):
    u = [t[2 * i] + s[0] * t[2 * i + 1] for i in range(4)]
    v = [u[0] + s[1] * u[1], u[2] + s[1] * u[3]]
    return v[0] + s[2] * v[1]


def unfold(w, s):
    a = [w, s[2] * w]
    b = [a[0], s[1] * a[0], a[1], s[1] * a[1]]
    return [e for p in b for e in (p, s[0] * p)]


def comm_kernel(
    g, res_in, bits_in, picks_in, tot, newres,
    res, bits, picks, gbuf, cin, kb, kept_o, kept_m, kcin, rsin, zin, y1in, x1in, x2in, y2in,
    isem, lsem, ksend, krecv, csend, crecv, rsend, rrecv, zsend, zrecv, asend, arecv,
    tsend, trecv, y1s, y1r, x1s, x1r, x2s, x2r, y2s, y2r,
):
    x, y, zg, zp, c = place()
    xh, xl = x // 2, x % 2
    oc = 1 - c
    mine = xh * 4 + y
    other_core = device(x, y, zg, zp, oc)

    def near(i):
        dx, dy, dp = i // 8, (i // 2) % 4, i % 2
        return (x + dx) % 4, (y + dy) % 4, (zp + dp) % 2

    def copy(src, dst, ssem, rsem, dev):
        cp = pltpu.make_async_remote_copy(
            src_ref=src, dst_ref=dst, send_sem=ssem, recv_sem=rsem, device_id=dev, device_id_type=MESH
        )
        cp.start()

    def wait(ref, sem):
        pltpu.make_async_copy(ref, ref, sem).wait()

    bar = pltpu.get_barrier_semaphore()

    def greet(dev):
        pl.semaphore_signal(bar, inc=1, device_id=dev, device_id_type=MESH)

    def greet_far(i, _):
        greet(device(x, y, (zg + i) % 8, zp, c))
        return 0

    def greet_near(i, _):
        px, py, pp = near(i)
        greet(device(px, py, zg, pp, c))
        return 0

    small = [(picks_in, picks), (bits_in, bits), (res_in, res)]
    small = [pltpu.make_async_copy(a, b, isem.at[i]) for i, (a, b) in enumerate(small)]
    small[0].start()
    small[1].start()
    lax.fori_loop(1, 8, greet_far, 0)
    lax.fori_loop(1, 32, greet_near, 0)
    greet(other_core)

    def load(s, core):
        r = rows((s * 2 + core) * SHARD, SHARD, SHARD)
        return pltpu.make_async_copy(g.at[r], gbuf.at[r], lsem.at[s * 2 + core])

    for s in range(8):
        load(s, oc).start()
    for s in range(8):
        load(s, c).start()

    small[2].start()

    small[0].wait()
    small[1].wait()
    for t in range(8):
        kb[t * LANES : (t + 1) * LANES, :] = spread_index(picks[t : t + 1, :])
    sgn = (1 - 2 * bits[...]).astype(F32)
    sg = [sgn[j : j + 1, :] for j in range(8)]

    def fold_rows(ref, row0, block0):
        t = [ref[pl.ds(row0 + j, 8, stride=8), :] * sg[j] for j in range(8)]
        return fold(t, flips(kb[rows(block0, 8, 8), :]))

    def fold_shard(s, core, dst):
        def body(i, _):
            row0 = pl.multiple_of((s * 2 + core) * SHARD + i * 64, 64)
            dst[rows(s * 64 + i * 8, 8, 8), :] = fold_rows(gbuf, row0, (s * 2 + core) * 64 + i * 8)
            return 0

        lax.fori_loop(0, 8, body, 0, unroll=4)

    for s in range(8):
        load(s, oc).wait()
        fold_shard(s, oc, kept_o)

    pl.semaphore_wait(bar, 39)

    copy(kept_o, kcin, ksend, krecv, other_core)
    for s in range(8):
        r = rows((s * 2 + oc) * SHARD, SHARD, SHARD)
        copy(gbuf.at[r], cin.at[s * SHARD : (s + 1) * SHARD], csend.at[s], crecv.at[s], other_core)

    for s in range(8):
        load(s, c).wait()
        fold_shard(s, c, kept_m)

    small[2].wait()

    def add_residual(i, _):
        r = rows(mine * 64 + i * 8, 8, 8)
        kept_m[r, :] += fold_rows(res, i * 64, (mine * 2 + c) * 64 + i * 8)
        return 0

    lax.fori_loop(0, 8, add_residual, 0)

    wait(kcin, krecv)

    def add_kept(i, _):
        r = rows(i * 64, 64, 64)
        kept_m[r, :] += kcin[r, :]
        return 0

    lax.fori_loop(0, 8, add_kept, 0)

    def chunk_row(px, py, pp):
        return ((px // 2) * 4 + py) * 64 + ((px % 2) * 2 + pp) * CHUNK

    def send_chunk(i, _):
        px, py, pp = near(i)
        copy(
            kept_m.at[rows(chunk_row(px, py, pp), CHUNK, CHUNK)],
            rsin.at[rows(i * CHUNK, CHUNK, CHUNK)],
            rsend, rrecv, device(px, py, zg, pp, c),
        )
        return 0

    lax.fori_loop(1, 32, send_chunk, 0)

    def own_row(s):
        return (s * 2 + c) * SHARD

    def add_core(s):
        wait(cin.at[s * SHARD : (s + 1) * SHARD], crecv.at[s])

        def body(i, _):
            r = rows(own_row(s) + i * 64, 64, 64)
            gbuf[r, :] += cin[rows(s * SHARD + i * 64, 64, 64), :]
            return 0

        lax.fori_loop(0, 8, body, 0)

    for s in range(8):
        add_core(s)

    rest = SHARD - FIRST
    across = device(x + 2 - 4 * xh, y, zg, zp, c)

    def along(dy):
        return device(x, (y + dy) % 4, zg, zp, c)

    for dy in (2, 1, 3):
        py = (y + dy) % 4
        for h in range(2):
            copy(
                gbuf.at[rows(own_row(h * 4 + py), FIRST, 16)],
                y1in.at[pl.ds(((dy - 1) * 2 + h) * FIRST, FIRST)],
                y1s.at[dy - 1], y1r.at[dy - 1], along(dy),
            )
    for py in range(4):
        copy(
            gbuf.at[rows(own_row((1 - xh) * 4 + py) + FIRST, rest, 16)],
            x1in.at[pl.ds(py * rest, rest)],
            x1s, x1r, across,
        )

    wait(rsin.at[CHUNK:], rrecv)
    my_row = chunk_row(x, y, zp)
    total = kept_m[rows(my_row, CHUNK, CHUNK), :]
    for i in range(1, 32):
        total = total + rsin[i * CHUNK : (i + 1) * CHUNK, :]
    zin[rows(zg * CHUNK, CHUNK, CHUNK), :] = total

    def send_far(i, _):
        r = rows(zg * CHUNK, CHUNK, CHUNK)
        copy(zin.at[r], zin.at[r], zsend, zrecv, device(x, y, (zg + i) % 8, zp, c))
        return 0

    lax.fori_loop(1, 8, send_far, 0)

    wait(x1in, x1r)
    for py in range(4):
        def body(i, _, py=py):
            r = rows(own_row(xh * 4 + py) + FIRST + i * 16, 16, 16)
            gbuf[r, :] += x1in[rows(py * rest + i * 16, 16, 16), :]
            return 0

        lax.fori_loop(0, rest // 16, body, 0, unroll=4)
    for dy in (2, 1, 3):
        copy(
            gbuf.at[rows(own_row(xh * 4 + (y + dy) % 4) + FIRST, rest, 16)],
            y2in.at[pl.ds((dy - 1) * rest, rest)],
            y2s.at[dy - 1], y2r.at[dy - 1], along(dy),
        )
    for dy in (1, 2, 3):
        wait(y1in.at[pl.ds((dy - 1) * 2 * FIRST, 2 * FIRST)], y1r.at[dy - 1])
    for h in range(2):
        def body(i, _, h=h):
            r = rows(own_row(h * 4 + y) + i * 16, 16, 16)
            a = [y1in[rows((2 * k + h) * FIRST + i * 16, 16, 16), :] for k in range(3)]
            gbuf[r, :] += a[0] + a[1] + a[2]
            return 0

        lax.fori_loop(0, FIRST // 16, body, 0, unroll=2)
    copy(gbuf.at[rows(own_row((1 - xh) * 4 + y), FIRST, 16)], x2in, x2s, x2r, across)

    wait(zin.at[0 : 7 * CHUNK], zrecv)
    z = [zin[i * CHUNK : (i + 1) * CHUNK, :] for i in range(8)]
    chunk = rows(c * 512 + my_row, CHUNK, CHUNK)
    tot[chunk, :] = ((z[0] + z[1]) + (z[2] + z[3])) + ((z[4] + z[5]) + (z[6] + z[7]))

    def send_total(i, _):
        px, py, pp = near(i)
        copy(tot.at[chunk], tot.at[chunk], asend, arecv, device(px, py, zg, pp, c))
        return 0

    lax.fori_loop(1, 32, send_total, 0)

    wait(x2in, x2r)
    for dy in (1, 2, 3):
        wait(y2in.at[pl.ds((dy - 1) * rest, rest)], y2r.at[dy - 1])
    base = own_row(mine)

    def add_x(i, _):
        r = rows(base + i * 16, 16, 16)
        gbuf[r, :] += x2in[rows(i * 16, 16, 16), :] + res[rows(i * 16, 16, 16), :]
        return 0

    lax.fori_loop(0, FIRST // 16, add_x, 0)

    def add_y(i, _):
        r = rows(base + FIRST + i * 16, 16, 16)
        a = [y2in[rows(k * rest + i * 16, 16, 16), :] for k in range(3)]
        gbuf[r, :] += (a[0] + a[1]) + (a[2] + res[rows(FIRST + i * 16, 16, 16), :])
        return 0

    lax.fori_loop(0, rest // 16, add_y, 0)

    def subtract(i, _):
        row0 = pl.multiple_of(base + i * 64, 64)
        t = [gbuf[pl.ds(row0 + j, 8, stride=8), :] for j in range(8)]
        s = flips(kb[rows((mine * 2 + c) * 64 + i * 8, 8, 8), :])
        w = fold([t[j] * sg[j] for j in range(8)], s) * 0.125
        for j, e in enumerate(unfold(w, s)):
            newres[pl.ds(pl.multiple_of(i * 64, 64) + j, 8, stride=8), :] = t[j] - e * sg[j]
        return 0

    lax.fori_loop(0, 8, subtract, 0)

    wait(tot.at[0 : 31 * CHUNK], arecv)
    half = rows(c * 512, 512, 512)
    copy(tot.at[half], tot.at[half], tsend, trecv, other_core)
    wait(tot.at[half], trecv)

    wait(kept_o, ksend)
    for s in range(8):
        wait(cin.at[s * SHARD : (s + 1) * SHARD], csend.at[s])
    wait(rsin.at[CHUNK:], rsend)
    wait(zin.at[0 : 7 * CHUNK], zsend)
    wait(tot.at[0 : 31 * CHUNK], asend)
    wait(tot.at[half], tsend)
    for dy in (1, 2, 3):
        wait(y1in.at[pl.ds((dy - 1) * 2 * FIRST, 2 * FIRST)], y1s.at[dy - 1])
        wait(y2in.at[pl.ds((dy - 1) * rest, rest)], y2s.at[dy - 1])
    wait(x1in, x1s)
    wait(x2in, x2s)


def decode_kernel(tot, bits, picks, res_in, synced, res_out):
    step = pl.program_id(0)
    res_out[...] = res_in[...]
    sgn = (1 - 2 * bits[...]).astype(F32)
    k = spread_index(picks[pl.ds(step, 1), :])
    for core in range(2):
        for i in range(8):
            at = core * 64 + i * 8
            w = tot[core, i * 8 : (i + 1) * 8, :] * (1.0 / 256.0)
            for j, e in enumerate(unfold(w, flips(k[at : at + 8, :]))):
                synced[pl.ds(at * 8 + j, 8, stride=8), :] = e * sgn[j : j + 1, :]


def shards(grads, residual, sign_bits, kept_index):
    g = grads.reshape(8192, LANES)
    res = residual.reshape(SHARD, LANES)
    bits = sign_bits.reshape(8, LANES)
    picks = kept_index.reshape(8, LANES)
    rest = SHARD - FIRST
    vmem = pl.BlockSpec(memory_space=pltpu.VMEM)
    dma = pltpu.SemaphoreType.DMA

    def buf(n, kind=F32):
        return pltpu.VMEM((n, LANES), kind)

    tot, newres = pl.pallas_call(
        comm_kernel,
        name="sum_pods",
        out_shape=(jax.ShapeDtypeStruct((1024, LANES), F32), jax.ShapeDtypeStruct((SHARD, LANES), F32)),
        in_specs=[pl.BlockSpec(memory_space=pltpu.HBM)] * 4,
        out_specs=(vmem, vmem),
        scratch_shapes=[
            buf(512), buf(8, jnp.int32), buf(8, jnp.int32), buf(8192), buf(4096), buf(1024, jnp.int32), buf(512), buf(512), buf(512),
            buf(32 * CHUNK), buf(8 * CHUNK), buf(6 * FIRST), buf(4 * rest), buf(FIRST), buf(3 * rest),
            dma((3,)), dma((16,)), dma, dma, dma((8,)), dma((8,)), dma, dma, dma, dma, dma, dma,
            dma, dma, dma((3,)), dma((3,)), dma, dma, dma, dma, dma((3,)), dma((3,)),
        ],
        compiler_params=pltpu.CompilerParams(
            collective_id=0, has_side_effects=True, vmem_limit_bytes=60 << 20
        ),
    )(g, res, bits, picks)

    whole = pl.BlockSpec((8, LANES), lambda i: (0, 0))
    synced, new_residual = pl.pallas_call(
        decode_kernel,
        name="decode",
        grid=(8,),
        out_shape=(jax.ShapeDtypeStruct((8192, LANES), F32), jax.ShapeDtypeStruct((SHARD, LANES), F32)),
        in_specs=[
            pl.BlockSpec((2, 64, LANES), lambda i: (0, i, 0)),
            whole,
            whole,
            pl.BlockSpec((64, LANES), lambda i: (i, 0)),
        ],
        out_specs=(
            pl.BlockSpec((1024, LANES), lambda i: (i, 0)),
            pl.BlockSpec((64, LANES), lambda i: (i, 0)),
        ),
    )(tot.reshape(2, 512, LANES), bits, picks, newres)
    return synced.reshape(-1), new_residual.reshape(1, -1)


def solution(mesh):
    in_specs = (P("outer", "dev", None), P("outer", "dev"), P(), P())
    out_specs = (P(), P("outer", "dev"))
    return jax.shard_map(shards, mesh=mesh, in_specs=in_specs, out_specs=out_specs, check_vma=False)
```

```python
import jax
import jax.numpy as jnp
from jax import lax
from jax.experimental import pallas as pl
from jax.experimental.pallas import tpu as pltpu
from jax.sharding import PartitionSpec as P

MESH = pl.DeviceIdType.MESH
F32 = jnp.float32
LANES = 128
SHARD = 512
CHUNK = 16
X_FIRST = (1, 3, 5, 7)
Y_FIRST = (2, 4, 6)
NEAR = sorted(
    ((dx, dy, dp) for dx in range(4) for dy in range(4) for dp in range(2) if dx + dy + dp),
    key=lambda d: -(min(d[0], 4 - d[0]) + min(d[1], 4 - d[1]) + d[2]),
)
FAR = (4, 3, 5, 2, 6, 1, 7)


def rows(start, size, multiple):
    return pl.ds(pl.multiple_of(start, multiple), size)


def spread_index(row):
    return jnp.transpose(jnp.broadcast_to(row.astype(F32), (LANES, LANES))).astype(jnp.int32)


def row_signs(k):
    s = [(1 - 2 * ((k >> bit) & 1)).astype(F32) for bit in range(3)]
    s01 = s[0] * s[1]
    return [None, s[0], s[1], s01, s[2], s[0] * s[2], s[1] * s[2], s01 * s[2]]


def times(a, b):
    return a if b is None else a * b


def transform(t):
    for step in (1, 2, 4):
        out = [None] * 8
        for i in range(8):
            if i & step == 0:
                p, q = t[i], t[i | step]
                out[i], out[i | step] = (q, -q) if p is None else (p + q, p - q)
        t = out
    return t


def comm_kernel(
    g, res_in, bits_in, picks_in, tot, newres,
    res, bits, picks, gbuf, coef, cin, kb, rcoef, rsin, zin, y1in, x1in, x2in, y2in,
    isem, lsem, csend, crecv, rsend, rrecv, zsend, zrecv, asend, arecv,
    tsend, trecv, y1s, y1r, x1s, x1r, x2s, x2r, y2s, y2r,
):
    o, d = lax.axis_index("outer"), lax.axis_index("dev")
    xh, xl, zg, zp = d // 8, o // 16, (o % 16) // 2, o % 2
    y, c = (d // 2) % 4, d % 2
    oc = 1 - c
    mine = xh * 4 + y

    ys = [y] + [(y + i) % 4 for i in (1, 2, 3)]
    xs = [(xh, xl)] + [((xh + (xl + i) // 2) % 2, (xl + i) % 2) for i in (1, 2, 3)]
    zgs = [zg] + [(zg + i) % 8 for i in range(1, 8)]
    zps = [zp, 1 - zp]

    def device(dx=0, dy=0, dp=0, far=0, core=None):
        h, l = xs[dx]
        return (l * 16 + zgs[far] * 2 + zps[dp], h * 8 + ys[dy] * 2 + (c if core is None else core))

    other_core = device(core=oc)

    def copy(src, dst, ssem, rsem, dev):
        pltpu.make_async_remote_copy(
            src_ref=src, dst_ref=dst, send_sem=ssem, recv_sem=rsem, device_id=dev, device_id_type=MESH
        ).start()

    def wait(ref, sem):
        pltpu.make_async_copy(ref, ref, sem).wait()

    small = [(picks_in, picks), (bits_in, bits), (res_in, res)]
    small = [pltpu.make_async_copy(a, b, isem.at[i]) for i, (a, b) in enumerate(small)]

    def load(s, core):
        r = rows((s * 2 + core) * SHARD, SHARD, SHARD)
        return pltpu.make_async_copy(g.at[r], gbuf.at[r], lsem.at[s * 2 + core])

    small[0].start()
    small[1].start()
    for s in range(8):
        load(s, oc).start()
    for s in range(8):
        load(s, c).start()
    small[2].start()

    bar = pltpu.get_barrier_semaphore()

    def greet(dev):
        pl.semaphore_signal(bar, inc=1, device_id=dev, device_id_type=MESH)

    for i in FAR:
        greet(device(far=i))
    for step in NEAR:
        greet(device(*step))
    greet(other_core)

    small[0].wait()
    small[1].wait()
    for t in range(8):
        kb[t * LANES : (t + 1) * LANES, :] = spread_index(picks[t : t + 1, :])
    sgn = (1 - 2 * bits[...]).astype(F32)
    sg = [sgn[j : j + 1, :] for j in range(8)]

    def plane(core, m, start=0):
        return ((core * 8 + m) * 8) * 64 + start

    def spread(src, row0, block0):
        k = row_signs(kb[rows(block0, 8, 8), :])
        return transform([times(src[pl.ds(row0 + j, 8, stride=8), :] * sg[j], k[j]) for j in range(8)])

    def spread_shard(s, core):
        def body(i, _):
            row0 = pl.multiple_of((s * 2 + core) * SHARD + i * 64, 64)
            for m, e in enumerate(spread(gbuf, row0, (s * 2 + core) * 64 + i * 8)):
                coef[rows(plane(core, m, s * 64 + i * 8), 8, 8), :] = e
            return 0

        lax.fori_loop(0, 8, body, 0, unroll=2)

    def core_send(m):
        copy(
            coef.at[rows(plane(oc, m), 512, 512)], cin.at[m * 512 : (m + 1) * 512],
            csend.at[m], crecv.at[m], other_core,
        )

    def core_add(m):
        wait(cin.at[m * 512 : (m + 1) * 512], crecv.at[m])

        def body(i, _):
            coef[rows(plane(c, m, i * 64), 64, 64), :] += cin[rows(m * 512 + i * 64, 64, 64), :]
            return 0

        lax.fori_loop(0, 8, body, 0)

    def spread_residual():
        small[2].wait()

        def body(i, _):
            for m, e in enumerate(spread(res, pl.multiple_of(i * 64, 64), (mine * 2 + c) * 64 + i * 8)):
                rcoef[rows(m * 64 + i * 8, 8, 8), :] = e
            return 0

        lax.fori_loop(0, 8, body, 0, unroll=2)
        coef[rows(plane(c, 0, mine * 64), 64, 64), :] += rcoef[0:64, :]

    def chunk_row(dx=0, dy=0, dp=0):
        h, l = xs[dx]
        return (h * 4 + ys[dy]) * 64 + (l * 2 + zps[dp]) * CHUNK

    my_far = rows(zg * CHUNK, CHUNK, CHUNK)
    my_chunk = rows(c * 512 + chunk_row(), CHUNK, CHUNK)
    my_half = rows(c * 512, 512, 512)

    def sketch_near_send():
        for i, step in enumerate(NEAR):
            copy(
                coef.at[rows(plane(c, 0, chunk_row(*step)), CHUNK, CHUNK)],
                rsin.at[i * CHUNK : (i + 1) * CHUNK],
                rsend, rrecv, device(*step),
            )

    def sketch_far_send():
        wait(rsin, rrecv)
        total = coef[rows(plane(c, 0, chunk_row()), CHUNK, CHUNK), :]
        for i in range(31):
            total = total + rsin[i * CHUNK : (i + 1) * CHUNK, :]
        zin[my_far, :] = total
        for i in FAR:
            copy(zin.at[my_far], zin.at[my_far], zsend, zrecv, device(far=i))

    def sketch_total_send():
        wait(zin.at[0 : 7 * CHUNK], zrecv)
        z = [zin[i * CHUNK : (i + 1) * CHUNK, :] for i in range(8)]
        tot[my_chunk, :] = ((z[0] + z[1]) + (z[2] + z[3])) + ((z[4] + z[5]) + (z[6] + z[7]))
        for step in NEAR:
            copy(tot.at[my_chunk], tot.at[my_chunk], asend, arecv, device(*step))

    def sketch_half_send():
        wait(tot.at[0 : 31 * CHUNK], arecv)
        copy(tot.at[my_half], tot.at[my_half], tsend, trecv, other_core)

    def x_first_send(i):
        copy(
            coef.at[rows(plane(c, X_FIRST[i], (1 - xh) * 256), 256, 64)],
            x1in.at[i * 256 : (i + 1) * 256],
            x1s.at[i], x1r.at[i], device(dx=2),
        )

    def x_second_send(i):
        m = X_FIRST[i]
        wait(x1in.at[i * 256 : (i + 1) * 256], x1r.at[i])

        def body(k, _):
            coef[rows(plane(c, m, xh * 256 + k * 64), 64, 64), :] += x1in[rows(i * 256 + k * 64, 64, 64), :]
            return 0

        lax.fori_loop(0, 4, body, 0)
        for n, dy in enumerate((2, 1, 3)):
            copy(
                coef.at[rows(plane(c, m, (xh * 4 + ys[dy]) * 64), 64, 64)],
                y2in.at[(i * 3 + n) * 64 : (i * 3 + n + 1) * 64],
                y2s.at[i], y2r.at[i], device(dy=dy),
            )

    def y_first_send(i):
        for n, dy in enumerate((2, 1, 3)):
            for h in range(2):
                at = ((i * 3 + n) * 2 + h) * 64
                copy(
                    coef.at[rows(plane(c, Y_FIRST[i], (h * 4 + ys[dy]) * 64), 64, 64)],
                    y1in.at[at : at + 64],
                    y1s.at[i], y1r.at[i], device(dy=dy),
                )

    def y_second_send(i):
        m = Y_FIRST[i]
        wait(y1in.at[i * 384 : (i + 1) * 384], y1r.at[i])
        for h in range(2):
            a = [y1in[i * 384 + (2 * n + h) * 64 : i * 384 + (2 * n + h + 1) * 64, :] for n in range(3)]
            coef[rows(plane(c, m, (h * 4 + y) * 64), 64, 64), :] += a[0] + a[1] + a[2]
        copy(
            coef.at[rows(plane(c, m, ((1 - xh) * 4 + y) * 64), 64, 64)],
            x2in.at[i * 64 : (i + 1) * 64],
            x2s.at[i], x2r.at[i], device(dx=2),
        )

    def finish_residual():
        for i in range(len(X_FIRST)):
            wait(y2in.at[i * 192 : (i + 1) * 192], y2r.at[i])
        for i in range(len(Y_FIRST)):
            wait(x2in.at[i * 64 : (i + 1) * 64], x2r.at[i])

        def body(b, _):
            t = [None]
            for m in range(1, 8):
                e = coef[rows(plane(c, m, mine * 64 + b * 8), 8, 8), :] + rcoef[rows(m * 64 + b * 8, 8, 8), :]
                if m in X_FIRST:
                    i = X_FIRST.index(m)
                    a = [y2in[rows((i * 3 + n) * 64 + b * 8, 8, 8), :] for n in range(3)]
                    e = e + (a[0] + a[1] + a[2])
                else:
                    e = e + x2in[rows(Y_FIRST.index(m) * 64 + b * 8, 8, 8), :]
                t.append(e)
            k = row_signs(kb[rows((mine * 2 + c) * 64 + b * 8, 8, 8), :])
            for j, e in enumerate(transform(t)):
                newres[pl.ds(pl.multiple_of(b * 64, 64) + j, 8, stride=8), :] = times(e * (sg[j] * 0.125), k[j])
            return 0

        lax.fori_loop(0, 8, body, 0, unroll=2)

    for s in range(8):
        load(s, oc).wait()
        spread_shard(s, oc)
    pl.semaphore_wait(bar, 39)
    for m in range(8):
        core_send(m)
    for s in range(8):
        load(s, c).wait()
        spread_shard(s, c)
    spread_residual()
    core_add(0)
    sketch_near_send()
    for i in range(4):
        core_add(X_FIRST[i])
        x_first_send(i)
        if i < 3:
            core_add(Y_FIRST[i])
            y_first_send(i)
    sketch_far_send()
    x_second_send(0)
    y_second_send(0)
    x_second_send(1)
    y_second_send(1)
    x_second_send(2)
    y_second_send(2)
    x_second_send(3)
    sketch_total_send()
    finish_residual()
    sketch_half_send()
    wait(tot.at[my_half], trecv)

    for m in range(8):
        wait(cin.at[m * 512 : (m + 1) * 512], csend.at[m])
    wait(rsin, rsend)
    wait(zin.at[0 : 7 * CHUNK], zsend)
    wait(tot.at[0 : 31 * CHUNK], asend)
    wait(tot.at[my_half], tsend)
    for i in range(len(X_FIRST)):
        wait(x1in.at[i * 256 : (i + 1) * 256], x1s.at[i])
        wait(y2in.at[i * 192 : (i + 1) * 192], y2s.at[i])
    for i in range(len(Y_FIRST)):
        wait(y1in.at[i * 384 : (i + 1) * 384], y1s.at[i])
        wait(x2in.at[i * 64 : (i + 1) * 64], x2s.at[i])


def decode_kernel(tot, bits, picks, res_in, synced, res_out, kb, out, sem):
    res_copy = pltpu.make_async_copy(res_in, res_out, sem.at[8])
    res_copy.start()
    sgn = (1 - 2 * bits[...]).astype(F32)
    sg = [sgn[j : j + 1, :] for j in range(8)]

    def piece(s):
        at = pl.ds(s * 1024, 1024)
        return pltpu.make_async_copy(out.at[at], synced.at[at], sem.at[s])

    for s in range(8):
        kb[...] = spread_index(picks[s : s + 1, :])
        for core in range(2):

            def body(i, _, s=s, core=core):
                w = tot[rows(core * 512 + s * 64 + i * 8, 8, 8), :] * (1.0 / 256.0)
                row0 = pl.multiple_of((s * 2 + core) * SHARD + i * 64, 64)
                for j, e in enumerate(row_signs(kb[rows(core * 64 + i * 8, 8, 8), :])):
                    out[pl.ds(row0 + j, 8, stride=8), :] = times(w * sg[j], e)
                return 0

            lax.fori_loop(0, 8, body, 0, unroll=4)
        piece(s).start()
    for s in range(8):
        piece(s).wait()
    res_copy.wait()


def shards(grads, residual, sign_bits, kept_index):
    def in_hbm(a):
        return pltpu.with_memory_space_constraint(a, pltpu.HBM)

    g = in_hbm(grads.reshape(8192, LANES))
    res = in_hbm(residual.reshape(SHARD, LANES))
    bits = in_hbm(sign_bits.reshape(8, LANES))
    picks = in_hbm(kept_index.reshape(8, LANES))
    vmem = pl.BlockSpec(memory_space=pltpu.VMEM)
    hbm = pl.BlockSpec(memory_space=pltpu.HBM)
    dma = pltpu.SemaphoreType.DMA

    def buf(n, kind=F32):
        return pltpu.VMEM((n, LANES), kind)

    tot, newres = pl.pallas_call(
        comm_kernel,
        name="sum_pods",
        out_shape=(buf(1024), buf(SHARD)),
        in_specs=[hbm] * 4,
        out_specs=(vmem, vmem),
        scratch_shapes=[
            buf(512), buf(8, jnp.int32), buf(8, jnp.int32), buf(8192), buf(8192), buf(4096), buf(1024, jnp.int32), buf(512),
            buf(31 * CHUNK), buf(8 * CHUNK), buf(3 * 384), buf(4 * 256), buf(3 * 64), buf(4 * 192),
            dma((3,)), dma((16,)), dma((8,)), dma((8,)), dma, dma, dma, dma, dma, dma,
            dma, dma, dma((3,)), dma((3,)), dma((4,)), dma((4,)), dma((3,)), dma((3,)), dma((4,)), dma((4,)),
        ],
        compiler_params=pltpu.CompilerParams(
            collective_id=0, has_side_effects=True, vmem_limit_bytes=24 << 20
        ),
    )(g, res, bits, picks)

    synced, new_residual = pl.pallas_call(
        decode_kernel,
        name="decode",
        out_shape=(jax.ShapeDtypeStruct((8192, LANES), F32), jax.ShapeDtypeStruct((SHARD, LANES), F32)),
        in_specs=[vmem] * 4,
        out_specs=(hbm, hbm),
        scratch_shapes=[buf(LANES, jnp.int32), buf(8192), dma((9,))],
        compiler_params=pltpu.CompilerParams(vmem_limit_bytes=24 << 20),
    )(tot, sign_bits.reshape(8, LANES), kept_index.reshape(8, LANES), newres)
    return synced.reshape(-1), new_residual.reshape(1, -1)


def solution(mesh):
    in_specs = (P("outer", "dev", None), P("outer", "dev"), P(), P())
    out_specs = (P(), P("outer", "dev"))
    return jax.shard_map(shards, mesh=mesh, in_specs=in_specs, out_specs=out_specs, check_vma=False)
```

```python
import jax
import jax.numpy as jnp
from jax import lax
from jax.experimental import pallas as pl
from jax.experimental.pallas import tpu as pltpu
from jax.sharding import PartitionSpec as P

MESH = pl.DeviceIdType.MESH
F32 = jnp.float32
LANES = 128
SHARD = 512
CHUNK = 8
X_FIRST = (1, 3, 5, 7)
Y_FIRST = (2, 4, 6)
NEAR = sorted(
    ((dx, dy, dp) for dx in range(4) for dy in range(4) for dp in range(2) if dx + dy + dp),
    key=lambda d: -(min(d[0], 4 - d[0]) + min(d[1], 4 - d[1]) + d[2]),
)
FAR = (4, 3, 5, 2, 6, 1, 7)


def rows(start, size, multiple):
    return pl.ds(pl.multiple_of(start, multiple), size)


def spread_index(row):
    return jnp.transpose(jnp.broadcast_to(row.astype(F32), (LANES, LANES))).astype(jnp.int32)


def row_signs(k):
    s = [(1 - 2 * ((k >> bit) & 1)).astype(F32) for bit in range(3)]
    s01 = s[0] * s[1]
    return [None, s[0], s[1], s01, s[2], s[0] * s[2], s[1] * s[2], s01 * s[2]]


def times(a, b):
    return a if b is None else a * b


def transform(t):
    for step in (1, 2, 4):
        out = [None] * 8
        for i in range(8):
            if i & step == 0:
                p, q = t[i], t[i | step]
                out[i], out[i | step] = (q, -q) if p is None else (p + q, p - q)
        t = out
    return t


def comm_kernel(
    g, res_in, bits_in, picks_in, tot, newres,
    res, bits, picks, gbuf, coef, cin, kb, rcoef, rsin, zin, y1in, x1in, x2in, y2in,
    isem, lsem, relay1, relay2, upper, ksend, krecv, csend, crecv, rsend, rrecv, zsend, zrecv, asend, arecv,
    tsend, trecv, y1s, y1r, x1s, x1r, x2s, x2r, y2s, y2r,
):
    o, d = lax.axis_index("outer"), lax.axis_index("dev")
    xh, xl, zg, zp = d // 8, o // 16, (o % 16) // 2, o % 2
    y, c = (d // 2) % 4, d % 2
    oc = 1 - c
    mine = xh * 4 + y

    ys = [y] + [(y + i) % 4 for i in (1, 2, 3)]
    xs = [(xh, xl)] + [((xh + (xl + i) // 2) % 2, (xl + i) % 2) for i in (1, 2, 3)]
    zgs = [zg] + [(zg + i) % 8 for i in range(1, 8)]
    zps = [zp, 1 - zp]

    def device(dx=0, dy=0, dp=0, far=0, core=None):
        h, l = xs[dx]
        return (l * 16 + zgs[far] * 2 + zps[dp], h * 8 + ys[dy] * 2 + (c if core is None else core))

    other_core = device(core=oc)

    def copy(src, dst, ssem, rsem, dev):
        pltpu.make_async_remote_copy(
            src_ref=src, dst_ref=dst, send_sem=ssem, recv_sem=rsem, device_id=dev, device_id_type=MESH
        ).start()

    def wait(ref, sem):
        pltpu.make_async_copy(ref, ref, sem).wait()

    small = [(picks_in, picks), (bits_in, bits), (res_in, res)]
    small = [pltpu.make_async_copy(a, b, isem.at[i]) for i, (a, b) in enumerate(small)]

    def load(s, core):
        r = rows((s * 2 + core) * SHARD, SHARD, SHARD)
        return pltpu.make_async_copy(g.at[r], gbuf.at[r], lsem.at[s * 2 + core])

    small[0].start()
    small[1].start()
    for s in range(4):
        load(s, oc).start()
    small[2].start()
    for s in range(4):
        load(s, c).start()
    for s in range(4, 8):
        load(s, oc).start()
    for s in range(4, 8):
        load(s, c).start()

    bar = pltpu.get_barrier_semaphore()

    def signal(sem, dev):
        pl.semaphore_signal(sem, inc=1, device_id=dev, device_id_type=MESH)

    for step in NEAR:
        signal(bar, device(*step))
    signal(bar, other_core)

    upper_half, zq = zg // 4, zg % 4

    def layer(t):
        return (xl * 16 + t * 2 + zp, xh * 8 + y * 2 + c)

    def neighbours(below, above):
        pl.when(zq > 0)(below)
        pl.when(zq < 3)(above)

    neighbours(lambda: signal(bar, layer(zg - 1)), lambda: signal(bar, layer(zg + 1)))

    @pl.when(upper_half == 0)
    def _():
        for t in range(4, 8):
            signal(bar, layer(t))

    def enter():
        pl.semaphore_wait(bar, 32 + (zq + 3) // 4 + (6 - zq) // 4 + 4 * upper_half)
        neighbours(lambda: signal(relay1.at[1], layer(zg - 1)), lambda: signal(relay1.at[0], layer(zg + 1)))

        @pl.when(upper_half == 1)
        def _():
            for t in range(4):
                signal(upper, layer(t))

    def pass_on():
        neighbours(lambda: pl.semaphore_wait(relay1.at[0], 1), lambda: pl.semaphore_wait(relay1.at[1], 1))
        pl.when(zq == 1)(lambda: signal(relay2, layer(zg + 2)))
        pl.when(zq == 2)(lambda: signal(relay2, layer(zg - 2)))

    def hear_all():
        pl.when(zq == 0)(lambda: pl.semaphore_wait(relay2, 1))
        pl.when(zq == 3)(lambda: pl.semaphore_wait(relay2, 1))
        pl.when(upper_half == 0)(lambda: pl.semaphore_wait(upper, 4))

    small[0].wait()
    small[1].wait()
    for t in range(8):
        kb[t * LANES : (t + 1) * LANES, :] = spread_index(picks[t : t + 1, :])
    sgn = (1 - 2 * bits[...]).astype(F32)
    sg = [sgn[j : j + 1, :] for j in range(8)]

    def plane(core, m, start=0):
        return ((core * 8 + m) * 8) * 64 + start

    def fold_shard(s, core):
        def body(i, _):
            row0 = pl.multiple_of((s * 2 + core) * SHARD + i * 64, 64)
            e = fold(gbuf, row0, (s * 2 + core) * 64 + i * 8)
            coef[rows(plane(core, 0, s * 64 + i * 8), 8, 8), :] = e
            return 0

        lax.fori_loop(0, 8, body, 0, unroll=4)

    def fold(src, row0, block0):
        k = kb[rows(block0, 8, 8), :]
        t = [src[pl.ds(row0 + j, 8, stride=8), :] * sg[j] for j in range(8)]
        for bit in range(3):
            sign = (1 - 2 * ((k >> bit) & 1)).astype(F32)
            t = [t[i] + sign * t[i + 1] for i in range(0, len(t), 2)]
        return t[0]

    def spread(src, row0, block0):
        k = row_signs(kb[rows(block0, 8, 8), :])
        return transform([times(src[pl.ds(row0 + j, 8, stride=8), :] * sg[j], k[j]) for j in range(8)])

    def spread_shard(s, core):
        def body(i, _):
            row0 = pl.multiple_of((s * 2 + core) * SHARD + i * 64, 64)
            for m, e in enumerate(spread(gbuf, row0, (s * 2 + core) * 64 + i * 8)[1:], 1):
                coef[rows(plane(core, m, s * 64 + i * 8), 8, 8), :] = e
            return 0

        lax.fori_loop(0, 8, body, 0, unroll=2)

    def core_send(m):
        copy(
            coef.at[rows(plane(oc, m), 512, 512)], cin.at[m * 512 : (m + 1) * 512],
            csend.at[m], crecv.at[m], other_core,
        )

    def core_add(m):
        wait(cin.at[m * 512 : (m + 1) * 512], crecv.at[m])

        def body(i, _):
            coef[rows(plane(c, m, i * 64), 64, 64), :] += cin[rows(m * 512 + i * 64, 64, 64), :]
            return 0

        lax.fori_loop(0, 8, body, 0)

    def spread_residual():
        def body(i, _):
            for m, e in enumerate(spread(res, pl.multiple_of(i * 64, 64), (mine * 2 + c) * 64 + i * 8)):
                rcoef[rows(m * 64 + i * 8, 8, 8), :] = e
            return 0

        lax.fori_loop(0, 8, body, 0, unroll=2)

    def chunk_row(dx=0, dy=0, dp=0):
        h, l = xs[dx]
        return ((h * 4 + ys[dy]) * 4 + l * 2 + zps[dp]) * CHUNK

    def half(q):
        return pl.ds(q * 256, 256)

    def far_rows(q):
        return rows((q * 8 + zg) * CHUNK, CHUNK, CHUNK)

    def total_chunk(q):
        return rows(c * 512 + q * 256 + chunk_row(), CHUNK, CHUNK)

    def total_half(q):
        return rows(c * 512 + q * 256, 256, 256)

    def sketch_core_send(q):
        copy(coef.at[rows(plane(oc, 0, q * 256), 256, 256)], cin.at[half(q)], ksend.at[q], krecv.at[q], other_core)

    def sketch_core_add(q):
        wait(cin.at[half(q)], krecv.at[q])
        for s in range(4 * q, 4 * q + 4):
            at = rows(plane(c, 0, s * 64), 64, 64)
            own = jnp.where(mine == s, 1.0, 0.0).astype(F32)
            coef[at, :] += cin[s * 64 : (s + 1) * 64, :] + own * rcoef[0:64, :]

    def sketch_near_send(q):
        for i, step in enumerate(NEAR):
            at = (q * 31 + i) * CHUNK
            copy(
                coef.at[rows(plane(c, 0, q * 256 + chunk_row(*step)), CHUNK, CHUNK)],
                rsin.at[at : at + CHUNK],
                rsend.at[q], rrecv.at[q], device(*step),
            )

    def sketch_far_send(q):
        wait(rsin.at[q * 31 * CHUNK : (q + 1) * 31 * CHUNK], rrecv.at[q])
        total = coef[rows(plane(c, 0, q * 256 + chunk_row()), CHUNK, CHUNK), :]
        for i in range(31):
            total = total + rsin[(q * 31 + i) * CHUNK : (q * 31 + i + 1) * CHUNK, :]
        zin[far_rows(q), :] = total
        for i in FAR:
            copy(zin.at[far_rows(q)], zin.at[far_rows(q)], zsend.at[q], zrecv.at[q], device(far=i))

    def sketch_total_send(q):
        wait(zin.at[q * 8 * CHUNK : (q * 8 + 7) * CHUNK], zrecv.at[q])
        z = [zin[(q * 8 + i) * CHUNK : (q * 8 + i + 1) * CHUNK, :] for i in range(8)]
        tot[total_chunk(q), :] = ((z[0] + z[1]) + (z[2] + z[3])) + ((z[4] + z[5]) + (z[6] + z[7]))
        for step in NEAR:
            copy(tot.at[total_chunk(q)], tot.at[total_chunk(q)], asend.at[q], arecv.at[q], device(*step))

    def sketch_half_send(q):
        wait(tot.at[0 : 31 * CHUNK], arecv.at[q])
        copy(tot.at[total_half(q)], tot.at[total_half(q)], tsend.at[q], trecv.at[q], other_core)

    def x_first_send(i):
        copy(
            coef.at[rows(plane(c, X_FIRST[i], (1 - xh) * 256), 256, 64)],
            x1in.at[i * 256 : (i + 1) * 256],
            x1s.at[i], x1r.at[i], device(dx=2),
        )

    def x_second_send(i):
        m = X_FIRST[i]
        wait(x1in.at[i * 256 : (i + 1) * 256], x1r.at[i])

        def body(k, _):
            coef[rows(plane(c, m, xh * 256 + k * 64), 64, 64), :] += x1in[rows(i * 256 + k * 64, 64, 64), :]
            return 0

        lax.fori_loop(0, 4, body, 0)
        for n, dy in enumerate((2, 1, 3)):
            copy(
                coef.at[rows(plane(c, m, (xh * 4 + ys[dy]) * 64), 64, 64)],
                y2in.at[(i * 3 + n) * 64 : (i * 3 + n + 1) * 64],
                y2s.at[i], y2r.at[i], device(dy=dy),
            )

    def y_first_send(i):
        for n, dy in enumerate((2, 1, 3)):
            for h in range(2):
                at = ((i * 3 + n) * 2 + h) * 64
                copy(
                    coef.at[rows(plane(c, Y_FIRST[i], (h * 4 + ys[dy]) * 64), 64, 64)],
                    y1in.at[at : at + 64],
                    y1s.at[i], y1r.at[i], device(dy=dy),
                )

    def y_second_send(i):
        m = Y_FIRST[i]
        wait(y1in.at[i * 384 : (i + 1) * 384], y1r.at[i])
        for h in range(2):
            a = [y1in[i * 384 + (2 * n + h) * 64 : i * 384 + (2 * n + h + 1) * 64, :] for n in range(3)]
            coef[rows(plane(c, m, (h * 4 + y) * 64), 64, 64), :] += a[0] + a[1] + a[2]
        copy(
            coef.at[rows(plane(c, m, ((1 - xh) * 4 + y) * 64), 64, 64)],
            x2in.at[i * 64 : (i + 1) * 64],
            x2s.at[i], x2r.at[i], device(dx=2),
        )

    def finish_residual():
        for i in range(len(X_FIRST)):
            wait(y2in.at[i * 192 : (i + 1) * 192], y2r.at[i])
        for i in range(len(Y_FIRST)):
            wait(x2in.at[i * 64 : (i + 1) * 64], x2r.at[i])

        def body(b, _):
            t = [None]
            for m in range(1, 8):
                e = coef[rows(plane(c, m, mine * 64 + b * 8), 8, 8), :] + rcoef[rows(m * 64 + b * 8, 8, 8), :]
                if m in X_FIRST:
                    i = X_FIRST.index(m)
                    a = [y2in[rows((i * 3 + n) * 64 + b * 8, 8, 8), :] for n in range(3)]
                    e = e + (a[0] + a[1] + a[2])
                else:
                    e = e + x2in[rows(Y_FIRST.index(m) * 64 + b * 8, 8, 8), :]
                t.append(e)
            k = row_signs(kb[rows((mine * 2 + c) * 64 + b * 8, 8, 8), :])
            for j, e in enumerate(transform(t)):
                newres[pl.ds(pl.multiple_of(b * 64, 64) + j, 8, stride=8), :] = times(e * (sg[j] * 0.125), k[j])
            return 0

        lax.fori_loop(0, 8, body, 0, unroll=2)

    for q in range(2):
        for s in range(4 * q, 4 * q + 4):
            load(s, oc).wait()
            fold_shard(s, oc)
        if q == 0:
            enter()
        sketch_core_send(q)
        for s in range(4 * q, 4 * q + 4):
            load(s, c).wait()
            fold_shard(s, c)
        if q == 0:
            small[2].wait()
            spread_residual()
        sketch_core_add(q)
        sketch_near_send(q)
    pass_on()
    for s in range(8):
        spread_shard(s, oc)
    for m in range(1, 8):
        core_send(m)
    for s in range(8):
        spread_shard(s, c)
    for i in range(4):
        core_add(X_FIRST[i])
        x_first_send(i)
        if i < 3:
            core_add(Y_FIRST[i])
            y_first_send(i)
    hear_all()
    sketch_far_send(0)
    sketch_far_send(1)
    for i in range(4):
        x_second_send(i)
        if i < 3:
            y_second_send(i)
    sketch_total_send(0)
    sketch_total_send(1)
    finish_residual()
    sketch_half_send(0)
    sketch_half_send(1)
    wait(tot.at[total_half(0)], trecv.at[0])
    wait(tot.at[total_half(1)], trecv.at[1])

    for q in range(2):
        wait(cin.at[half(q)], ksend.at[q])
        wait(rsin.at[q * 31 * CHUNK : (q + 1) * 31 * CHUNK], rsend.at[q])
        wait(zin.at[0 : 7 * CHUNK], zsend.at[q])
        wait(tot.at[0 : 31 * CHUNK], asend.at[q])
        wait(tot.at[total_half(q)], tsend.at[q])
    for m in range(1, 8):
        wait(cin.at[m * 512 : (m + 1) * 512], csend.at[m])
    for i in range(len(X_FIRST)):
        wait(x1in.at[i * 256 : (i + 1) * 256], x1s.at[i])
        wait(y2in.at[i * 192 : (i + 1) * 192], y2s.at[i])
    for i in range(len(Y_FIRST)):
        wait(y1in.at[i * 384 : (i + 1) * 384], y1s.at[i])
        wait(x2in.at[i * 64 : (i + 1) * 64], x2s.at[i])


def decode_kernel(tot, bits, picks, res_in, synced, res_out, kb, out, sem):
    res_copy = pltpu.make_async_copy(res_in, res_out, sem.at[8])
    res_copy.start()
    sgn = (1 - 2 * bits[...]).astype(F32)
    sg = [sgn[j : j + 1, :] for j in range(8)]

    def piece(s):
        at = pl.ds(s * 1024, 1024)
        return pltpu.make_async_copy(out.at[at], synced.at[at], sem.at[s])

    for s in range(8):
        kb[...] = spread_index(picks[s : s + 1, :])
        for core in range(2):

            def body(i, _, s=s, core=core):
                w = tot[rows(core * 512 + s * 64 + i * 8, 8, 8), :] * (1.0 / 256.0)
                row0 = pl.multiple_of((s * 2 + core) * SHARD + i * 64, 64)
                for j, e in enumerate(row_signs(kb[rows(core * 64 + i * 8, 8, 8), :])):
                    out[pl.ds(row0 + j, 8, stride=8), :] = times(w * sg[j], e)
                return 0

            lax.fori_loop(0, 8, body, 0, unroll=4)
        piece(s).start()
    for s in range(8):
        piece(s).wait()
    res_copy.wait()


def shards(grads, residual, sign_bits, kept_index):
    def in_hbm(a):
        return pltpu.with_memory_space_constraint(a, pltpu.HBM)

    g = in_hbm(grads.reshape(8192, LANES))
    res = in_hbm(residual.reshape(SHARD, LANES))
    bits = in_hbm(sign_bits.reshape(8, LANES))
    picks = in_hbm(kept_index.reshape(8, LANES))
    vmem = pl.BlockSpec(memory_space=pltpu.VMEM)
    hbm = pl.BlockSpec(memory_space=pltpu.HBM)
    dma = pltpu.SemaphoreType.DMA

    def buf(n, kind=F32):
        return pltpu.VMEM((n, LANES), kind)

    tot, newres = pl.pallas_call(
        comm_kernel,
        name="sum_pods",
        out_shape=(buf(1024), buf(SHARD)),
        in_specs=[hbm] * 4,
        out_specs=(vmem, vmem),
        scratch_shapes=[
            buf(512), buf(8, jnp.int32), buf(8, jnp.int32), buf(8192), buf(8192), buf(4096), buf(1024, jnp.int32), buf(512),
            buf(62 * CHUNK), buf(16 * CHUNK), buf(3 * 384), buf(4 * 256), buf(3 * 64), buf(4 * 192),
            dma((3,)), dma((16,)), pltpu.SemaphoreType.REGULAR((2,)), pltpu.SemaphoreType.REGULAR, pltpu.SemaphoreType.REGULAR,
            dma((2,)), dma((2,)), dma((8,)), dma((8,)), dma((2,)), dma((2,)), dma((2,)), dma((2,)), dma((2,)), dma((2,)),
            dma((2,)), dma((2,)), dma((3,)), dma((3,)), dma((4,)), dma((4,)), dma((3,)), dma((3,)), dma((4,)), dma((4,)),
        ],
        compiler_params=pltpu.CompilerParams(
            collective_id=0, has_side_effects=True, vmem_limit_bytes=24 << 20
        ),
    )(g, res, bits, picks)

    synced, new_residual = pl.pallas_call(
        decode_kernel,
        name="decode",
        out_shape=(jax.ShapeDtypeStruct((8192, LANES), F32), jax.ShapeDtypeStruct((SHARD, LANES), F32)),
        in_specs=[vmem] * 4,
        out_specs=(hbm, hbm),
        scratch_shapes=[buf(LANES, jnp.int32), buf(8192), dma((9,))],
        compiler_params=pltpu.CompilerParams(vmem_limit_bytes=24 << 20),
    )(tot, sign_bits.reshape(8, LANES), kept_index.reshape(8, LANES), newres)
    return synced.reshape(-1), new_residual.reshape(1, -1)


def solution(mesh):
    in_specs = (P("outer", "dev", None), P("outer", "dev"), P(), P())
    out_specs = (P(), P("outer", "dev"))
    return jax.shard_map(shards, mesh=mesh, in_specs=in_specs, out_specs=out_specs, check_vma=False)
```
